32 devices in a mesh: parts: 2 (over y), dp: 8 (over z, x), mp: 2 (over core).
Axes of the slice: x: 2, y: 2, z: 4, core: 2. Of those that a mesh axis runs over, the one named last changes fastest.
Arguments:
- embeddings: bfloat16 [6144, 1024], P(('parts', 'dp'), 'mp'), parts along dimension 0, may hold values from -6 to 6
- labels: int32 [6144], P(('parts', 'dp')), parts along dimension 0, may hold values from 0 to 1023, as said below
- block_lists: int32 [2048, 2], P(('parts', 'dp')), parts along dimension 0, may hold values from -1 to 3, as said below
- level1: bfloat16 [16384, 1024], P(('parts', 'dp'), 'mp'), parts along dimension 0, may hold values from -6 to 6
- level2: bfloat16 [2048, 1024], P(('parts', 'dp'), 'mp'), parts along dimension 0, may hold values from -6 to 6
- level3: bfloat16 [512, 1024], P('parts', 'mp'), parts along dimension 0, may hold values from -6 to 6
Outputs:
- new_level1: bfloat16 [16384, 1024], P(('parts', 'dp'), 'mp'), parts along dimension 0
- new_level2: bfloat16 [2048, 1024], P(('parts', 'dp'), 'mp'), parts along dimension 0
- new_level3: bfloat16 [512, 1024], P('parts', 'mp'), parts along dimension 0
The draws below stay inside these ranges and needn't reach their ends.
There are 2 independent parts, one for each index of `parts`. The reference program is written for one: setup_inputs(seed, part) draws one part's arguments, and reference() takes and returns one part's arrays. A program takes and returns all parts, laid end to end along the dimension named above; each array names one. Nothing has to cross between parts.
Inputs may be any that keep to these rules, and one draw needn't show every extreme that they name: Among the 384 embeddings of one index of dp, at most 96 have labels of one owner (label // 128), and exactly 96 for some owner on every index. `block_lists`: each row holds distinct block numbers followed by -1 padding; its first entry is never -1.
All inputs are finite; a program needn't handle non-finite values.
Results may differ from the reference program's by a relative error of at most 0.004.
Values may be sent and summed in bfloat16 or wider, within the bound.
A program may use at most 64 MiB of HBM per device.

```python
import jax
import jax.numpy as jnp
from jax import lax

E = 1024
BR = 256
BLK_DEV = 4
L = 2
K2_DEV = 128
K3 = 256
ROWS_DEV = 384
ROWS = 3072
SLOTS = 768
K1 = 8192
K2 = 1024
N_DP = 8


def draw_labels(key, part):
    key = jax.random.fold_in(key, 11)
    cap = max(2, 2 * ROWS_DEV // N_DP)
    slots = N_DP * cap
    key_hot, key_rows = jax.random.split(key)
    penalty = jax.random.randint(key_hot, (N_DP,), 0, slots)
    dest = jnp.arange(slots) // cap

    def one_device(subkey):
        key_a, key_b, key_c = jax.random.split(subkey, 3)
        ranked = jax.random.permutation(key_a, slots)
        filled = jax.random.randint(key_b, (), 0, N_DP)
        score = ranked + penalty[dest]
        score = jnp.where(dest == filled, -1 - jnp.arange(slots), score)
        order = jnp.argsort(score, stable=True)[:ROWS_DEV]
        local = jax.random.randint(key_c, (ROWS_DEV,), 0, K2_DEV)
        return (dest[order] * K2_DEV + local).astype(jnp.int32)
    drawn = jax.vmap(one_device)(jax.random.split(key_rows, N_DP))
    return drawn.reshape(ROWS_DEV * N_DP)


def draw_block_lists(key, part):
    key = jax.random.fold_in(key, 12)
    key_perm, key_count = jax.random.split(key)
    perms = jax.vmap(lambda sub: jax.random.permutation(sub, BLK_DEV)[:L])(jax.random.split(key_perm, K2))
    count = jax.random.randint(key_count, (K2, 1), 1, L + 1)
    return jnp.where(jnp.arange(L)[None, :] < count, perms, -1).astype(jnp.int32)


def drawn_rows(key, count):
    return jnp.clip(jax.random.normal(key, (count, E), jnp.float32), -6.0, 6.0)


def draw_embeddings(key, part):
    rows = drawn_rows(jax.random.fold_in(key, 14), ROWS)
    return rows.astype(jnp.bfloat16)


def draw_level1(key, part):
    rows = drawn_rows(jax.random.fold_in(key, 13), K1)
    return rows.astype(jnp.bfloat16)


def draw_level2(key, part):
    rows = drawn_rows(jax.random.fold_in(key, 15), K2)
    return rows.astype(jnp.bfloat16)


def draw_level3(key, part):
    rows = drawn_rows(jax.random.fold_in(key, 16), K3)
    return rows.astype(jnp.bfloat16)


def setup_inputs(seed: int = 0, part: int = 0) -> dict:
    keys = jax.random.split(jax.random.key(seed), 7)
    part_splits = jax.random.split(jax.random.fold_in(keys[6], part), 7)
    return {
        "embeddings": draw_embeddings(jax.random.fold_in(jax.random.fold_in(keys[6], part), 71), part),
        "labels": draw_labels(jax.random.fold_in(jax.random.fold_in(keys[6], part), 71), part),
        "block_lists": draw_block_lists(jax.random.fold_in(jax.random.fold_in(keys[6], part), 71), part),
        "level1": draw_level1(jax.random.fold_in(jax.random.fold_in(keys[6], part), 71), part),
        "level2": draw_level2(jax.random.fold_in(jax.random.fold_in(keys[6], part), 71), part),
        "level3": draw_level3(jax.random.fold_in(jax.random.fold_in(keys[6], part), 71), part),
    }


def soft_weights(scores, mask):
    top = jnp.max(jnp.where(mask, scores, -1e30), axis=1, keepdims=True)
    expd = jnp.where(mask, jnp.exp(scores - top), 0.0)
    total = jnp.sum(expd, axis=1, keepdims=True)
    total = jnp.where(total > 0, total, 1.0)
    return (expd / total).astype(jnp.bfloat16)


def reference(embeddings, labels, block_lists, level1, level2, level3):
    scale = float(E) ** -0.5
    owner = labels // K2_DEV
    cents = level1.reshape(N_DP, BLK_DEV * BR, E)
    lists = block_lists.reshape(N_DP, K2_DEV, L)
    seconds = level2.reshape(N_DP, K2_DEV, E)

    def per_owner(args):
        dest, cent, lst, sec = args
        picked = owner == dest
        idx = jnp.nonzero(picked, size=SLOTS, fill_value=0)[0].astype(jnp.int32)
        valid = jnp.arange(SLOTS) < jnp.sum(picked.astype(jnp.int32))
        rows = embeddings[idx]
        lab = jnp.where(valid, labels[idx] - dest * K2_DEV, -1)
        label_hot = lab[:, None] == jnp.arange(K2_DEV)[None, :]
        listed = jnp.any(lst[:, :, None] == jnp.arange(BLK_DEV)[None, None, :], axis=1).astype(jnp.float32)
        allowed = jnp.dot(label_hot.astype(jnp.float32), listed) > 0.5
        mask = jnp.repeat(allowed, BR, axis=1)
        cent_f = cent.astype(jnp.float32)
        norms = jnp.sum(cent_f * cent_f, axis=1)
        scores = (jnp.dot(rows, cent.T, preferred_element_type=jnp.float32) - 0.5 * norms[None, :]) * scale
        resp = soft_weights(scores, mask)
        num = jnp.dot(resp.T, rows, preferred_element_type=jnp.float32)
        weight = jnp.sum(resp.astype(jnp.float32), axis=0)
        new1 = ((num + cent_f) / (weight + 1.0)[:, None]).astype(jnp.bfloat16)
        member = label_hot.astype(jnp.bfloat16)
        sums = jnp.dot(member.T, rows, preferred_element_type=jnp.float32)
        count = jnp.sum(label_hot.astype(jnp.float32), axis=0)
        new2 = ((sums + sec.astype(jnp.float32)) / (count + 1.0)[:, None]).astype(jnp.bfloat16)
        return new1, new2

    new1, new2 = lax.map(per_owner, (jnp.arange(N_DP, dtype=jnp.int32), cents, lists, seconds))
    new1 = new1.reshape(K1, E)
    new2 = new2.reshape(K2, E)
    third = level3.astype(jnp.float32)
    norms3 = jnp.sum(third * third, axis=1)
    scores3 = (jnp.dot(new2, level3.T, preferred_element_type=jnp.float32) - 0.5 * norms3[None, :]) * scale
    resp3 = jax.nn.softmax(scores3, axis=1).astype(jnp.bfloat16)
    num3 = jnp.dot(resp3.T, new2, preferred_element_type=jnp.float32)
    weight3 = jnp.sum(resp3.astype(jnp.float32), axis=0)
    new3 = ((num3 + third) / (weight3 + 1.0)[:, None]).astype(jnp.bfloat16)
    return new1, new2, new3
```

```python
import functools

import jax
import jax.numpy as jnp
from jax import lax
from jax.experimental import pallas as pl
from jax.experimental.pallas import tpu as pltpu
from jax.sharding import PartitionSpec as P

E = 1024
BR = 256
BLK_DEV = 4


def soft_weights(scores, mask):
    top = jnp.max(jnp.where(mask, scores, -1e30), axis=1, keepdims=True)
    expd = jnp.where(mask, jnp.exp(scores - top), 0.0)
    total = jnp.sum(expd, axis=1, keepdims=True)
    total = jnp.where(total > 0, total, 1.0)
    return (expd / total).astype(jnp.bfloat16)


def plain_shards(embeddings, labels, block_lists, level1, level2, level3):
    scale = float(E) ** (-0.5)
    groups = lax.axis_size("dp")
    rows, half = embeddings.shape
    k2_local = level2.shape[0]
    cap = max(2, 2 * rows // groups)
    slots = groups * cap
    dest = labels // k2_local
    dest_hot = (dest[:, None] == jnp.arange(groups)[None, :]).astype(jnp.int32)
    rank = jnp.sum(dest_hot * (jnp.cumsum(dest_hot, axis=0) - 1), axis=1)
    target = dest * cap + rank
    sent_rows = jnp.zeros((slots, half), jnp.bfloat16).at[target].set(embeddings)
    sent_labels = jnp.full((slots,), -1, jnp.int32).at[target].set(labels - dest * k2_local)
    got_rows, got_labels = (
        lax.all_to_all(
            sent_rows.reshape(groups, cap, half), "dp", split_axis=0, concat_axis=0, tiled=True
        ),
        lax.all_to_all(
            sent_labels.reshape(groups, cap), "dp", split_axis=0, concat_axis=0, tiled=True
        ),
    )
    got_rows = got_rows.reshape(slots, half)
    got_labels = got_labels.reshape(slots)
    label_hot = got_labels[:, None] == jnp.arange(k2_local)[None, :]
    listed = jnp.any(block_lists[:, :, None] == jnp.arange(BLK_DEV)[None, None, :], axis=1).astype(
        jnp.float32
    )
    allowed = jnp.dot(label_hot.astype(jnp.float32), listed) > 0.5
    mask = jnp.repeat(allowed, BR, axis=1)
    cent_f = level1.astype(jnp.float32)
    norms = jnp.sum(cent_f * cent_f, axis=1)
    partial_value = (
        jnp.dot(got_rows, level1.T, preferred_element_type=jnp.float32) - 0.5 * norms[None, :]
    )
    scores = lax.psum(partial_value, "mp") * scale
    resp = soft_weights(scores, mask)
    num = jnp.dot(resp.T, got_rows, preferred_element_type=jnp.float32)
    weight = jnp.sum(resp.astype(jnp.float32), axis=0)
    new_level1 = ((num + cent_f) / (weight + 1.0)[:, None]).astype(jnp.bfloat16)
    member = label_hot.astype(jnp.bfloat16)
    sums = jnp.dot(member.T, got_rows, preferred_element_type=jnp.float32)
    count = jnp.sum(label_hot.astype(jnp.float32), axis=0)
    new_level2 = ((sums + level2.astype(jnp.float32)) / (count + 1.0)[:, None]).astype(jnp.bfloat16)
    third = level3.astype(jnp.float32)
    norms3 = jnp.sum(third * third, axis=1)
    partial3 = (
        jnp.dot(new_level2, level3.T, preferred_element_type=jnp.float32) - 0.5 * norms3[None, :]
    )
    scores3 = lax.psum(partial3, "mp") * scale
    resp3 = jax.nn.softmax(scores3, axis=1).astype(jnp.bfloat16)
    num3 = jnp.dot(resp3.T, new_level2, preferred_element_type=jnp.float32)
    weight3 = jnp.sum(resp3.astype(jnp.float32), axis=0)
    total3, mass3 = lax.psum((num3, weight3), "dp")
    new_level3 = ((total3 + third) / (mass3 + 1.0)[:, None]).astype(jnp.bfloat16)
    return (new_level1, new_level2, new_level3)


MESH = pl.DeviceIdType.MESH
NT = (((1,), (1,)), ((), ()))


def dot_nt(a, b):
    return lax.dot_general(a, b, NT, preferred_element_type=jnp.float32)


def dot_nn(a, b):
    return jnp.dot(a, b, preferred_element_type=jnp.float32)


def partner_order(groups):
    half = groups // 2
    order = []
    for step in range(half):
        for offset in (half + step, half - step):
            if 0 < offset < groups and offset not in order:
                order.append(offset)
    return [0] + order


def step_kernel(
    groups, cap, emb, lab, lists, l1, l2, l3, o1, o2, o3,
    sent, sent_lab, got, got_peer, got_lab, l1_peer, l3_peer, half_norm, half_norm3,
    num, mass, sums, count, listed, n2, n2_peer, part3, w3, got3, got_w3, n3,
    one_send, one_recv, row_send, row_recv, lab_send, lab_recv, fwd_send, fwd_recv,
    sum_send, sum_recv, w_send, w_recv, end_send, end_recv,
):
    me = lax.axis_index("dp")
    other = 1 - lax.axis_index("mp")
    rows = emb.shape[0]
    k2 = l2.shape[0]
    k3 = l3.shape[0]
    k1 = l1.shape[0]
    seg = k3 // groups
    scale = float(E) ** (-0.5)
    order = partner_order(groups)

    def to_owner(offset):
        return lax.rem(me + offset, groups)

    barrier = pltpu.get_barrier_semaphore()
    for offset in range(1, groups):
        pl.semaphore_signal(barrier, inc=1, device_id={"dp": to_owner(offset)}, device_id_type=MESH)
    pl.semaphore_signal(barrier, inc=1, device_id={"mp": other}, device_id_type=MESH)

    label = lab[...]
    at = me + lax.broadcasted_iota(jnp.int32, (groups, rows), 0)
    first = jnp.where(at >= groups, at - groups, at) * k2
    here = (label >= first) & (label < first + k2)
    upper = lax.broadcasted_iota(jnp.int32, (rows, rows), 0) <= lax.broadcasted_iota(
        jnp.int32, (rows, rows), 1
    )
    upper = jnp.where(upper, 1.0, 0.0).astype(jnp.bfloat16)
    cum = dot_nn(jnp.where(here, 1.0, 0.0).astype(jnp.bfloat16), upper).astype(jnp.int32)
    key = jnp.where(here, cum - 1, -1)
    local = jnp.where(here, label - first + 1, 0).astype(jnp.float32)

    def peer_copy(src, dst, index):
        return pltpu.make_async_remote_copy(
            src_ref=src, dst_ref=dst, send_sem=one_send.at[index], recv_sem=one_recv.at[index],
            device_id={"mp": other}, device_id_type=MESH,
        )

    def row_copy(slot, offset):
        return pltpu.make_async_remote_copy(
            src_ref=sent.at[slot], dst_ref=got.at[slot],
            send_sem=row_send.at[slot], recv_sem=row_recv.at[slot],
            device_id={"dp": to_owner(offset)}, device_id_type=MESH,
        )

    def lab_copy(slot, offset):
        return pltpu.make_async_remote_copy(
            src_ref=sent_lab.at[slot], dst_ref=got_lab.at[slot],
            send_sem=lab_send.at[slot], recv_sem=lab_recv.at[slot],
            device_id={"dp": to_owner(offset)}, device_id_type=MESH,
        )

    def forward(slot):
        return pltpu.make_async_remote_copy(
            src_ref=got.at[slot], dst_ref=got_peer.at[slot],
            send_sem=fwd_send.at[slot], recv_sem=fwd_recv.at[slot],
            device_id={"mp": other}, device_id_type=MESH,
        )

    def route(slot):
        offset = order[slot]
        spot = lax.broadcasted_iota(jnp.int32, (128, rows), 0) == key[offset : offset + 1]
        spot = jnp.where(spot, 1.0, 0.0).astype(jnp.bfloat16)
        names = jnp.broadcast_to(local[offset : offset + 1], (8, rows)).astype(jnp.bfloat16)
        return dot_nn(spot[:cap], emb[...]).astype(jnp.bfloat16), dot_nt(names, spot)

    for slot in range(1, groups):
        block, names = route(slot)
        sent[slot] = block
        sent_lab[slot] = names
        if slot == 1:
            pl.semaphore_wait(barrier, groups)
        lab_copy(slot, order[slot]).start()
        row_copy(slot, order[slot]).start()
    l1_copy = peer_copy(l1, l1_peer, 0)
    l3_copy = peer_copy(l3, l3_peer, 1)
    block, names = route(0)
    got[0] = block
    got_lab[0] = names
    forward(0).start()
    l1_copy.start()
    l3_copy.start()

    block_of = lax.broadcasted_iota(jnp.int32, (16, k2), 0)
    hit = lists[0:1] == block_of
    for entry in range(1, lists.shape[0]):
        hit = hit | (lists[entry : entry + 1] == block_of)
    listed[...] = jnp.where(hit, 1.0, 0.0).astype(jnp.bfloat16)
    num[...] = jnp.zeros_like(num)
    mass[...] = jnp.zeros_like(mass)
    sums[...] = jnp.zeros_like(sums)
    count[...] = jnp.zeros_like(count)

    def own_norms(x):
        x = x.astype(jnp.float32)
        return 0.5 * jnp.sum(x * x, axis=1, keepdims=True)

    half_norm[...] = own_norms(l1[...])
    norms3 = own_norms(l3[...])
    l1_copy.wait()
    l3_copy.wait()
    half_norm[...] += own_norms(l1_peer[...])
    norms3 = norms3 + own_norms(l3_peer[...])
    half_norm3[...] = jnp.broadcast_to(norms3, (k3, 128)).T

    def hot(slot):
        names = got_lab[slot][0:1, :cap].astype(jnp.int32) - 1
        return lax.broadcasted_iota(jnp.int32, (k2, cap), 0) == names

    def level2_part(slot):
        member = jnp.where(hot(slot), 1.0, 0.0)
        sums[...] += dot_nn(member.astype(jnp.bfloat16), got[slot])
        count[...] += member

    def level1_part(slot):
        own = got[slot]
        peer = got_peer[slot]
        member = jnp.where(hot(slot), 1.0, 0.0).astype(jnp.bfloat16)
        allowed = dot_nn(listed[...], member)
        top = jnp.full((1, cap), -1e30, jnp.float32)
        scores = []
        masks = []
        for b in range(BLK_DEV):
            span = pl.ds(b * BR, BR)
            score = (dot_nt(l1[span], own) + dot_nt(l1_peer[span], peer) - half_norm[span]) * scale
            mask = jnp.broadcast_to(allowed[b : b + 1], (BR, cap)) > 0.5
            top = jnp.maximum(top, jnp.max(jnp.where(mask, score, -1e30), axis=0, keepdims=True))
            scores.append(score)
            masks.append(mask)
        total = jnp.zeros((1, cap), jnp.float32)
        for b in range(BLK_DEV):
            scores[b] = jnp.where(masks[b], jnp.exp(scores[b] - top), 0.0)
            total = total + jnp.sum(scores[b], axis=0, keepdims=True)
        inverse = 1.0 / jnp.where(total > 0, total, 1.0)
        for b in range(BLK_DEV):
            span = pl.ds(b * BR, BR)
            resp = (scores[b] * inverse).astype(jnp.bfloat16)
            num[span] += dot_nn(resp, own)
            mass[span] += resp.astype(jnp.float32)

    level2_part(0)

    def one_slot(slot, carry):
        lab_copy(slot, 0).wait_recv()
        row_copy(slot, 0).wait_recv()
        forward(slot).start()
        level2_part(slot)
        forward(slot - 1).wait_recv()
        level1_part(slot - 1)
        return carry

    lax.fori_loop(1, groups - 1, one_slot, 0)
    last = groups - 1
    lab_copy(last, 0).wait_recv()
    row_copy(last, 0).wait_recv()
    forward(last).start()
    level2_part(last)
    members = jnp.sum(count[...], axis=1, keepdims=True)
    new2 = ((sums[...] + l2[...].astype(jnp.float32)) / (members + 1.0)).astype(jnp.bfloat16)
    n2[...] = new2
    n2_copy = peer_copy(n2, n2_peer, 2)
    n2_copy.start()
    o2[...] = new2
    forward(last - 1).wait_recv()
    level1_part(last - 1)
    n2_copy.wait()

    scores3 = dot_nt(n2[...], l3[...]) + dot_nt(n2_peer[...], l3_peer[...])
    norm_row = half_norm3[...]
    scores3 = (scores3 - norm_row[0:1]) * scale
    top3 = jnp.max(scores3, axis=1, keepdims=True)
    exp3 = jnp.exp(scores3 - top3)
    resp3 = exp3 / jnp.sum(exp3, axis=1, keepdims=True)
    resp3 = resp3.astype(jnp.bfloat16).astype(jnp.float32)
    part3[...] = dot_nn(resp3.T.astype(jnp.bfloat16), n2[...])
    w3[...] = jnp.broadcast_to(jnp.sum(resp3, axis=0, keepdims=True), (8, k3))

    def share(owner):
        return pl.ds(pl.multiple_of(owner * seg, seg), seg)

    def sum_copy(slot, offset):
        return pltpu.make_async_remote_copy(
            src_ref=part3.at[share(to_owner(offset))], dst_ref=got3.at[slot],
            send_sem=sum_send.at[slot], recv_sem=sum_recv.at[slot],
            device_id={"dp": to_owner(offset)}, device_id_type=MESH,
        )

    def w_copy(slot, offset):
        return pltpu.make_async_remote_copy(
            src_ref=w3, dst_ref=got_w3.at[slot],
            send_sem=w_send.at[slot], recv_sem=w_recv.at[slot],
            device_id={"dp": to_owner(offset)}, device_id_type=MESH,
        )

    def end_copy(slot, offset):
        return pltpu.make_async_remote_copy(
            src_ref=n3.at[share(me)], dst_ref=n3.at[share(me)],
            send_sem=end_send.at[slot], recv_sem=end_recv.at[slot],
            device_id={"dp": to_owner(offset)}, device_id_type=MESH,
        )

    for slot in range(1, groups):
        w_copy(slot, order[slot]).start()
        sum_copy(slot, order[slot]).start()

    forward(last).wait_recv()
    level1_part(last)
    for b in range(BLK_DEV):
        span = pl.ds(b * BR, BR)
        weight = jnp.sum(mass[span], axis=1, keepdims=True)
        o1[span] = ((num[span] + l1[span].astype(jnp.float32)) / (weight + 1.0)).astype(jnp.bfloat16)

    total3 = part3[share(me)]
    mass3 = w3[...]
    for slot in range(1, groups):
        w_copy(slot, order[slot]).wait_recv()
        sum_copy(slot, order[slot]).wait_recv()
        total3 = total3 + got3[slot]
        mass3 = mass3 + got_w3[slot]
    mine = lax.broadcasted_iota(jnp.int32, (seg, k3), 1) == me * seg + lax.broadcasted_iota(
        jnp.int32, (seg, k3), 0
    )
    mass_own = jnp.sum(jnp.where(mine, mass3[0:1], 0.0), axis=1, keepdims=True)
    new3 = (total3 + l3[share(me)].astype(jnp.float32)) / (mass_own + 1.0)
    n3[share(me)] = new3.astype(jnp.bfloat16)
    for slot in range(1, groups):
        end_copy(slot, order[slot]).start()
    for slot in range(1, groups):
        lab_copy(slot, order[slot]).wait_send()
        row_copy(slot, order[slot]).wait_send()
        w_copy(slot, order[slot]).wait_send()
        sum_copy(slot, order[slot]).wait_send()
    for slot in range(groups):
        forward(slot).wait_send()
    for slot in range(1, groups):
        end_copy(slot, order[slot]).wait_recv()
    o3[...] = n3[...]
    for slot in range(1, groups):
        end_copy(slot, order[slot]).wait_send()


def shards(embeddings, labels, block_lists, level1, level2, level3):
    groups = lax.axis_size("dp")
    rows, half = embeddings.shape
    k1, k2, k3 = level1.shape[0], level2.shape[0], level3.shape[0]
    cap = max(2, 2 * rows // groups)
    if cap % 16 or cap > 128 or groups % 8 or k3 % (16 * groups):
        return plain_shards(embeddings, labels, block_lists, level1, level2, level3)
    vmem = pl.BlockSpec(memory_space=pltpu.VMEM)
    bf16, f32 = jnp.bfloat16, jnp.float32
    dma = pltpu.SemaphoreType.DMA
    seg = k3 // groups
    return pl.pallas_call(
        functools.partial(step_kernel, groups, cap),
        out_shape=(
            jax.ShapeDtypeStruct((k1, half), bf16),
            jax.ShapeDtypeStruct((k2, half), bf16),
            jax.ShapeDtypeStruct((k3, half), bf16),
        ),
        in_specs=[vmem] * 6,
        out_specs=(vmem,) * 3,
        scratch_shapes=[
            pltpu.VMEM((groups, cap, half), bf16),
            pltpu.VMEM((groups, 8, 128), f32),
            pltpu.VMEM((groups, cap, half), bf16),
            pltpu.VMEM((groups, cap, half), bf16),
            pltpu.VMEM((groups, 8, 128), f32),
            pltpu.VMEM((k1, half), bf16),
            pltpu.VMEM((k3, half), bf16),
            pltpu.VMEM((k1, 1), f32),
            pltpu.VMEM((128, k3), f32),
            pltpu.VMEM((k1, half), f32),
            pltpu.VMEM((k1, cap), f32),
            pltpu.VMEM((k2, half), f32),
            pltpu.VMEM((k2, cap), f32),
            pltpu.VMEM((16, k2), bf16),
            pltpu.VMEM((k2, half), bf16),
            pltpu.VMEM((k2, half), bf16),
            pltpu.VMEM((k3, half), f32),
            pltpu.VMEM((8, k3), f32),
            pltpu.VMEM((groups, seg, half), f32),
            pltpu.VMEM((groups, 8, k3), f32),
            pltpu.VMEM((k3, half), bf16),
            dma((3,)),
            dma((3,)),
        ]
        + [dma((groups,))] * 12,
        compiler_params=pltpu.CompilerParams(
            collective_id=0, has_side_effects=True, vmem_limit_bytes=40 * 1024 * 1024
        ),
    )(embeddings, labels.reshape(1, rows), block_lists.T, level1, level2, level3)


def solution(mesh):
    return jax.shard_map(
        shards,
        mesh=mesh,
        in_specs=(
            P(("parts", "dp"), "mp"),
            P(("parts", "dp")),
            P(("parts", "dp"), None),
            P(("parts", "dp"), "mp"),
            P(("parts", "dp"), "mp"),
            P("parts", "mp"),
        ),
        out_specs=(P(("parts", "dp"), "mp"), P(("parts", "dp"), "mp"), P("parts", "mp")),
        check_vma=False,
    )
```

```python
import functools

import jax
import jax.numpy as jnp
from jax import lax
from jax.experimental import pallas as pl
from jax.experimental.pallas import tpu as pltpu
from jax.sharding import PartitionSpec as P

E = 1024
BR = 256
BLK_DEV = 4


def soft_weights(scores, mask):
    top = jnp.max(jnp.where(mask, scores, -1e30), axis=1, keepdims=True)
    expd = jnp.where(mask, jnp.exp(scores - top), 0.0)
    total = jnp.sum(expd, axis=1, keepdims=True)
    total = jnp.where(total > 0, total, 1.0)
    return (expd / total).astype(jnp.bfloat16)


def plain_shards(embeddings, labels, block_lists, level1, level2, level3):
    scale = float(E) ** (-0.5)
    groups = lax.axis_size("dp")
    rows, half = embeddings.shape
    k2_local = level2.shape[0]
    cap = max(2, 2 * rows // groups)
    slots = groups * cap
    dest = labels // k2_local
    dest_hot = (dest[:, None] == jnp.arange(groups)[None, :]).astype(jnp.int32)
    rank = jnp.sum(dest_hot * (jnp.cumsum(dest_hot, axis=0) - 1), axis=1)
    target = dest * cap + rank
    sent_rows = jnp.zeros((slots, half), jnp.bfloat16).at[target].set(embeddings)
    sent_labels = jnp.full((slots,), -1, jnp.int32).at[target].set(labels - dest * k2_local)
    got_rows, got_labels = (
        lax.all_to_all(
            sent_rows.reshape(groups, cap, half), "dp", split_axis=0, concat_axis=0, tiled=True
        ),
        lax.all_to_all(
            sent_labels.reshape(groups, cap), "dp", split_axis=0, concat_axis=0, tiled=True
        ),
    )
    got_rows = got_rows.reshape(slots, half)
    got_labels = got_labels.reshape(slots)
    label_hot = got_labels[:, None] == jnp.arange(k2_local)[None, :]
    listed = jnp.any(block_lists[:, :, None] == jnp.arange(BLK_DEV)[None, None, :], axis=1).astype(
        jnp.float32
    )
    allowed = jnp.dot(label_hot.astype(jnp.float32), listed) > 0.5
    mask = jnp.repeat(allowed, BR, axis=1)
    cent_f = level1.astype(jnp.float32)
    norms = jnp.sum(cent_f * cent_f, axis=1)
    partial_value = (
        jnp.dot(got_rows, level1.T, preferred_element_type=jnp.float32) - 0.5 * norms[None, :]
    )
    scores = lax.psum(partial_value, "mp") * scale
    resp = soft_weights(scores, mask)
    num = jnp.dot(resp.T, got_rows, preferred_element_type=jnp.float32)
    weight = jnp.sum(resp.astype(jnp.float32), axis=0)
    new_level1 = ((num + cent_f) / (weight + 1.0)[:, None]).astype(jnp.bfloat16)
    member = label_hot.astype(jnp.bfloat16)
    sums = jnp.dot(member.T, got_rows, preferred_element_type=jnp.float32)
    count = jnp.sum(label_hot.astype(jnp.float32), axis=0)
    new_level2 = ((sums + level2.astype(jnp.float32)) / (count + 1.0)[:, None]).astype(jnp.bfloat16)
    third = level3.astype(jnp.float32)
    norms3 = jnp.sum(third * third, axis=1)
    partial3 = (
        jnp.dot(new_level2, level3.T, preferred_element_type=jnp.float32) - 0.5 * norms3[None, :]
    )
    scores3 = lax.psum(partial3, "mp") * scale
    resp3 = jax.nn.softmax(scores3, axis=1).astype(jnp.bfloat16)
    num3 = jnp.dot(resp3.T, new_level2, preferred_element_type=jnp.float32)
    weight3 = jnp.sum(resp3.astype(jnp.float32), axis=0)
    total3, mass3 = lax.psum((num3, weight3), "dp")
    new_level3 = ((total3 + third) / (mass3 + 1.0)[:, None]).astype(jnp.bfloat16)
    return (new_level1, new_level2, new_level3)


MESH = pl.DeviceIdType.MESH
NT = (((1,), (1,)), ((), ()))


def dot_nt(a, b):
    return lax.dot_general(a, b, NT, preferred_element_type=jnp.float32)


def dot_nn(a, b):
    return jnp.dot(a, b, preferred_element_type=jnp.float32)


def partner_order(groups):
    half = groups // 2
    order = []
    for step in range(half):
        for offset in (half + step, half - step):
            if 0 < offset < groups and offset not in order:
                order.append(offset)
    return [0] + order[::-1]


def step_kernel(
    groups, cap, emb_hbm, lab_ref, lists, l1_hbm, l2_hbm, l3_hbm, o1_hbm, o2_hbm, o3_hbm,
    emb, l1, l2, l3, part3_own, o1, in_sem, out_sem,
    sent, sent_lab, got, got_peer, got_lab, l1_peer, l3_peer, half_norm, half_norm3,
    num, mass, sums, count, listed, n2, n2_peer, part3, w3, got3, got_w3, n3,
    one_send, one_recv, row_send, row_recv, lab_send, lab_recv, fwd_send, fwd_recv,
    sum_send, sum_recv, w_send, w_recv, end_send, end_recv,
):
    me = lax.axis_index("dp")
    other = 1 - lax.axis_index("mp")
    rows = emb.shape[0]
    k2 = l2.shape[0]
    k3 = l3.shape[0]
    k1 = l1.shape[0]
    seg = k3 // groups
    scale = float(E) ** (-0.5)
    order = partner_order(groups)

    def to_owner(offset):
        return lax.rem(me + offset, groups)

    def load(src, dst, index):
        return pltpu.make_async_copy(src, dst, in_sem.at[index])

    emb_load = load(emb_hbm, emb, 0)
    l1_load = load(l1_hbm, l1, 1)
    l2_load = load(l2_hbm, l2, 2)
    l3_load = load(l3_hbm, l3, 3)
    emb_load.start()
    barrier = pltpu.get_barrier_semaphore()
    for offset in range(1, groups):
        pl.semaphore_signal(barrier, inc=1, device_id={"dp": to_owner(offset)}, device_id_type=MESH)
    pl.semaphore_signal(barrier, inc=1, device_id={"mp": other}, device_id_type=MESH)

    l1_load.start()
    l3_load.start()
    l2_load.start()

    label = lab_ref[...].reshape(1, rows)
    at = me + lax.broadcasted_iota(jnp.int32, (groups, rows), 0)
    first = jnp.where(at >= groups, at - groups, at) * k2
    here = (label >= first) & (label < first + k2)
    upper = lax.broadcasted_iota(jnp.int32, (rows, rows), 0) <= lax.broadcasted_iota(
        jnp.int32, (rows, rows), 1
    )
    upper = jnp.where(upper, 1.0, 0.0).astype(jnp.bfloat16)
    cum = dot_nn(jnp.where(here, 1.0, 0.0).astype(jnp.bfloat16), upper).astype(jnp.int32)
    key = jnp.where(here, cum - 1, -1)
    local = jnp.where(here, label - first + 1, 0).astype(jnp.float32)

    def peer_copy(src, dst, index):
        return pltpu.make_async_remote_copy(
            src_ref=src, dst_ref=dst, send_sem=one_send.at[index], recv_sem=one_recv.at[index],
            device_id={"mp": other}, device_id_type=MESH,
        )

    def row_copy(slot, offset):
        return pltpu.make_async_remote_copy(
            src_ref=sent.at[slot], dst_ref=got.at[slot],
            send_sem=row_send.at[slot], recv_sem=row_recv.at[slot],
            device_id={"dp": to_owner(offset)}, device_id_type=MESH,
        )

    def lab_copy(slot, offset):
        return pltpu.make_async_remote_copy(
            src_ref=sent_lab.at[slot], dst_ref=got_lab.at[slot],
            send_sem=lab_send.at[slot], recv_sem=lab_recv.at[slot],
            device_id={"dp": to_owner(offset)}, device_id_type=MESH,
        )

    def forward(slot):
        return pltpu.make_async_remote_copy(
            src_ref=got.at[slot], dst_ref=got_peer.at[slot],
            send_sem=fwd_send.at[slot], recv_sem=fwd_recv.at[slot],
            device_id={"mp": other}, device_id_type=MESH,
        )

    def route(slot):
        offset = order[slot]
        spot = lax.broadcasted_iota(jnp.int32, (128, rows), 0) == key[offset : offset + 1]
        spot = jnp.where(spot, 1.0, 0.0).astype(jnp.bfloat16)
        names = jnp.broadcast_to(local[offset : offset + 1], (8, rows)).astype(jnp.bfloat16)
        return dot_nn(spot[:cap], emb[...]).astype(jnp.bfloat16), dot_nt(names, spot)[0:1]

    emb_load.wait()
    for slot in range(1, groups):
        block, names = route(slot)
        sent[slot] = block
        sent_lab[slot] = names
        if slot == 1:
            pl.semaphore_wait(barrier, groups)
        lab_copy(slot, order[slot]).start()
        row_copy(slot, order[slot]).start()
    l1_copy = peer_copy(l1_hbm, l1_peer, 0)
    l3_copy = peer_copy(l3_hbm, l3_peer, 1)
    block, names = route(0)
    got[0] = block
    got_lab[0] = names
    forward(0).start()
    l1_copy.start()
    l3_copy.start()

    block_of = lax.broadcasted_iota(jnp.int32, (16, k2), 0)
    hit = lists[0:1] == block_of
    for entry in range(1, lists.shape[0]):
        hit = hit | (lists[entry : entry + 1] == block_of)
    listed[...] = jnp.where(hit, 1.0, 0.0).astype(jnp.bfloat16)
    num[...] = jnp.zeros_like(num)
    mass[...] = jnp.zeros_like(mass)
    sums[...] = jnp.zeros_like(sums)
    count[...] = jnp.zeros_like(count)

    def own_norms(x):
        x = x.astype(jnp.float32)
        return 0.5 * jnp.sum(x * x, axis=1, keepdims=True)

    l1_load.wait()
    l3_load.wait()
    l2_load.wait()
    half_norm[...] = own_norms(l1[...])
    norms3 = own_norms(l3[...])
    l1_copy.wait()
    l3_copy.wait()
    half_norm[...] += own_norms(l1_peer[...])
    norms3 = norms3 + own_norms(l3_peer[...])
    half_norm3[...] = jnp.broadcast_to(norms3, (k3, 128)).T

    def hot(slot):
        names = got_lab[slot][0:1, :cap].astype(jnp.int32) - 1
        return lax.broadcasted_iota(jnp.int32, (k2, cap), 0) == names

    def level2_part(slot):
        member = jnp.where(hot(slot), 1.0, 0.0)
        sums[...] += dot_nn(member.astype(jnp.bfloat16), got[slot])
        count[...] += member

    def level1_part(slot):
        own = got[slot]
        peer = got_peer[slot]
        member = jnp.where(hot(slot), 1.0, 0.0).astype(jnp.bfloat16)
        allowed = dot_nn(listed[...], member)
        top = jnp.full((1, cap), -1e30, jnp.float32)
        scores = []
        masks = []
        for b in range(BLK_DEV):
            span = pl.ds(b * BR, BR)
            score = (dot_nt(l1[span], own) + dot_nt(l1_peer[span], peer) - half_norm[span]) * scale
            mask = jnp.broadcast_to(allowed[b : b + 1], (BR, cap)) > 0.5
            top = jnp.maximum(top, jnp.max(jnp.where(mask, score, -1e30), axis=0, keepdims=True))
            scores.append(score)
            masks.append(mask)
        total = jnp.zeros((1, cap), jnp.float32)
        for b in range(BLK_DEV):
            scores[b] = jnp.where(masks[b], jnp.exp(scores[b] - top), 0.0)
            total = total + jnp.sum(scores[b], axis=0, keepdims=True)
        inverse = 1.0 / jnp.where(total > 0, total, 1.0)
        for b in range(BLK_DEV):
            span = pl.ds(b * BR, BR)
            resp = (scores[b] * inverse).astype(jnp.bfloat16)
            num[span] += dot_nn(resp, own)
            mass[span] += resp.astype(jnp.float32)

    level2_part(0)

    def one_slot(slot, carry):
        lab_copy(slot, 0).wait_recv()
        row_copy(slot, 0).wait_recv()
        forward(slot).start()
        level2_part(slot)
        forward(slot - 1).wait_recv()
        level1_part(slot - 1)
        return carry

    lax.fori_loop(1, groups - 1, one_slot, 0)
    last = groups - 1
    lab_copy(last, 0).wait_recv()
    row_copy(last, 0).wait_recv()
    forward(last).start()
    level2_part(last)
    members = jnp.sum(count[...], axis=1, keepdims=True)
    new2 = ((sums[...] + l2[...].astype(jnp.float32)) / (members + 1.0)).astype(jnp.bfloat16)
    n2[...] = new2
    n2_copy = peer_copy(n2, n2_peer, 2)
    n2_copy.start()
    o2_copy = pltpu.make_async_copy(n2, o2_hbm, out_sem.at[BLK_DEV])
    o2_copy.start()
    forward(last - 1).wait_recv()
    level1_part(last - 1)
    n2_copy.wait()

    scores3 = dot_nt(n2[...], l3[...]) + dot_nt(n2_peer[...], l3_peer[...])
    norm_row = half_norm3[...]
    scores3 = (scores3 - norm_row[0:1]) * scale
    top3 = jnp.max(scores3, axis=1, keepdims=True)
    exp3 = jnp.exp(scores3 - top3)
    resp3 = exp3 / jnp.sum(exp3, axis=1, keepdims=True)
    resp3 = resp3.astype(jnp.bfloat16).astype(jnp.float32)
    sum3 = dot_nn(resp3.T.astype(jnp.bfloat16), n2[...])
    part3[...] = sum3.astype(jnp.bfloat16)
    part3_own[...] = sum3
    w3[...] = jnp.sum(resp3, axis=0, keepdims=True)

    def share(owner):
        return pl.ds(pl.multiple_of(owner * seg, seg), seg)

    def sum_copy(slot, offset):
        return pltpu.make_async_remote_copy(
            src_ref=part3.at[share(to_owner(offset))], dst_ref=got3.at[slot],
            send_sem=sum_send.at[slot], recv_sem=sum_recv.at[slot],
            device_id={"dp": to_owner(offset)}, device_id_type=MESH,
        )

    def w_copy(slot, offset):
        return pltpu.make_async_remote_copy(
            src_ref=w3, dst_ref=got_w3.at[slot],
            send_sem=w_send.at[slot], recv_sem=w_recv.at[slot],
            device_id={"dp": to_owner(offset)}, device_id_type=MESH,
        )

    def end_copy(slot, offset):
        return pltpu.make_async_remote_copy(
            src_ref=n3.at[share(me)], dst_ref=n3.at[share(me)],
            send_sem=end_send.at[slot], recv_sem=end_recv.at[slot],
            device_id={"dp": to_owner(offset)}, device_id_type=MESH,
        )

    for slot in range(1, groups):
        w_copy(slot, order[slot]).start()
        sum_copy(slot, order[slot]).start()

    forward(last).wait_recv()
    level1_part(last)
    o1_copies = []
    for b in range(BLK_DEV):
        span = pl.ds(b * BR, BR)
        weight = jnp.sum(mass[span], axis=1, keepdims=True)
        o1[span] = ((num[span] + l1[span].astype(jnp.float32)) / (weight + 1.0)).astype(jnp.bfloat16)
        copy = pltpu.make_async_copy(o1.at[span], o1_hbm.at[span], out_sem.at[b])
        copy.start()
        o1_copies.append(copy)

    total3 = part3_own[share(me)]
    mass3 = w3[...]
    for slot in range(1, groups):
        w_copy(slot, order[slot]).wait_recv()
        sum_copy(slot, order[slot]).wait_recv()
        total3 = total3 + got3[slot].astype(jnp.float32)
        mass3 = mass3 + got_w3[slot]
    mine = lax.broadcasted_iota(jnp.int32, (seg, k3), 1) == me * seg + lax.broadcasted_iota(
        jnp.int32, (seg, k3), 0
    )
    mass_own = jnp.sum(jnp.where(mine, mass3, 0.0), axis=1, keepdims=True)
    new3 = (total3 + l3[share(me)].astype(jnp.float32)) / (mass_own + 1.0)
    n3[share(me)] = new3.astype(jnp.bfloat16)
    for slot in range(1, groups):
        end_copy(slot, order[slot]).start()
    for slot in range(1, groups):
        lab_copy(slot, order[slot]).wait_send()
        row_copy(slot, order[slot]).wait_send()
        w_copy(slot, order[slot]).wait_send()
        sum_copy(slot, order[slot]).wait_send()
    for slot in range(groups):
        forward(slot).wait_send()
    for slot in range(1, groups):
        end_copy(slot, order[slot]).wait_recv()
    o3_copy = pltpu.make_async_copy(n3, o3_hbm, out_sem.at[BLK_DEV + 1])
    o3_copy.start()
    for copy in o1_copies:
        copy.wait()
    o2_copy.wait()
    for slot in range(1, groups):
        end_copy(slot, order[slot]).wait_send()
    o3_copy.wait()


def write_kernel(a, b, c, a_out, b_out, c_out, a_mid, b_mid, c_mid, in_sem, out_sem):
    pieces = []
    for index in range(BLK_DEV):
        span = pl.ds(index * BR, BR)
        pieces.append((a.at[span], a_mid.at[span], a_out.at[span]))
    pieces += [(b, b_mid, b_out), (c, c_mid, c_out)]
    reads, writes = [], []
    for index, (src, mid, dst) in enumerate(pieces):
        reads.append(pltpu.make_async_copy(src, mid, in_sem.at[index]))
        writes.append(pltpu.make_async_copy(mid, dst, out_sem.at[index]))
    for read in reads:
        read.start()
    for read, write in zip(reads, writes):
        read.wait()
        write.start()
    for write in writes:
        write.wait()


def shards(embeddings, labels, block_lists, level1, level2, level3):
    groups = lax.axis_size("dp")
    rows, half = embeddings.shape
    k1, k2, k3 = level1.shape[0], level2.shape[0], level3.shape[0]
    cap = max(2, 2 * rows // groups)
    if cap % 16 or cap > 128 or groups % 8 or k3 % (16 * groups):
        return plain_shards(embeddings, labels, block_lists, level1, level2, level3)
    vmem = pl.BlockSpec(memory_space=pltpu.VMEM)
    hbm = pl.BlockSpec(memory_space=pltpu.HBM)
    bf16, f32 = jnp.bfloat16, jnp.float32
    dma = pltpu.SemaphoreType.DMA
    seg = k3 // groups
    outs = pl.pallas_call(
        functools.partial(step_kernel, groups, cap),
        out_shape=(
            jax.ShapeDtypeStruct((k1, half), bf16),
            jax.ShapeDtypeStruct((k2, half), bf16),
            jax.ShapeDtypeStruct((k3, half), bf16),
        ),
        in_specs=[hbm, vmem, vmem, hbm, hbm, hbm],
        out_specs=(hbm,) * 3,
        scratch_shapes=[
            pltpu.VMEM((rows, half), bf16),
            pltpu.VMEM((k1, half), bf16),
            pltpu.VMEM((k2, half), bf16),
            pltpu.VMEM((k3, half), bf16),
            pltpu.VMEM((k3, half), f32),
            pltpu.VMEM((k1, half), bf16),
            dma((4,)),
            dma((BLK_DEV + 2,)),
            pltpu.VMEM((groups, cap, half), bf16),
            pltpu.VMEM((groups, 1, 128), f32),
            pltpu.VMEM((groups, cap, half), bf16),
            pltpu.VMEM((groups, cap, half), bf16),
            pltpu.VMEM((groups, 1, 128), f32),
            pltpu.VMEM((k1, half), bf16),
            pltpu.VMEM((k3, half), bf16),
            pltpu.VMEM((k1, 1), f32),
            pltpu.VMEM((128, k3), f32),
            pltpu.VMEM((k1, half), f32),
            pltpu.VMEM((k1, cap), f32),
            pltpu.VMEM((k2, half), f32),
            pltpu.VMEM((k2, cap), f32),
            pltpu.VMEM((16, k2), bf16),
            pltpu.VMEM((k2, half), bf16),
            pltpu.VMEM((k2, half), bf16),
            pltpu.VMEM((k3, half), bf16),
            pltpu.VMEM((1, k3), f32),
            pltpu.VMEM((groups, seg, half), bf16),
            pltpu.VMEM((groups, 1, k3), f32),
            pltpu.VMEM((k3, half), bf16),
            dma((3,)),
            dma((3,)),
        ]
        + [dma((groups,))] * 12,
        compiler_params=pltpu.CompilerParams(
            collective_id=0, has_side_effects=True, vmem_limit_bytes=60 * 1024 * 1024
        ),
    )(embeddings, labels, block_lists.T, level1, level2, level3)
    return pl.pallas_call(
        write_kernel,
        out_shape=tuple(jax.ShapeDtypeStruct(out.shape, out.dtype) for out in outs),
        in_specs=[hbm] * 3,
        out_specs=(hbm,) * 3,
        scratch_shapes=[pltpu.VMEM(out.shape, out.dtype) for out in outs]
        + [dma((BLK_DEV + 2,))] * 2,
        compiler_params=pltpu.CompilerParams(vmem_limit_bytes=60 * 1024 * 1024),
    )(*outs)


def solution(mesh):
    return jax.shard_map(
        shards,
        mesh=mesh,
        in_specs=(
            P(("parts", "dp"), "mp"),
            P(("parts", "dp")),
            P(("parts", "dp"), None),
            P(("parts", "dp"), "mp"),
            P(("parts", "dp"), "mp"),
            P("parts", "mp"),
        ),
        out_specs=(P(("parts", "dp"), "mp"), P(("parts", "dp"), "mp"), P("parts", "mp")),
        check_vma=False,
    )
```

```python
import functools

import jax
import jax.numpy as jnp
from jax import lax
from jax.experimental import pallas as pl
from jax.experimental.pallas import tpu as pltpu
from jax.sharding import PartitionSpec as P

E = 1024
BR = 256
BLK_DEV = 4


def soft_weights(scores, mask):
    top = jnp.max(jnp.where(mask, scores, -1e30), axis=1, keepdims=True)
    expd = jnp.where(mask, jnp.exp(scores - top), 0.0)
    total = jnp.sum(expd, axis=1, keepdims=True)
    total = jnp.where(total > 0, total, 1.0)
    return (expd / total).astype(jnp.bfloat16)


def plain_shards(embeddings, labels, block_lists, level1, level2, level3):
    scale = float(E) ** (-0.5)
    groups = lax.axis_size("dp")
    rows, half = embeddings.shape
    k2_local = level2.shape[0]
    cap = max(2, 2 * rows // groups)
    slots = groups * cap
    dest = labels // k2_local
    dest_hot = (dest[:, None] == jnp.arange(groups)[None, :]).astype(jnp.int32)
    rank = jnp.sum(dest_hot * (jnp.cumsum(dest_hot, axis=0) - 1), axis=1)
    target = dest * cap + rank
    sent_rows = jnp.zeros((slots, half), jnp.bfloat16).at[target].set(embeddings)
    sent_labels = jnp.full((slots,), -1, jnp.int32).at[target].set(labels - dest * k2_local)
    got_rows, got_labels = (
        lax.all_to_all(
            sent_rows.reshape(groups, cap, half), "dp", split_axis=0, concat_axis=0, tiled=True
        ),
        lax.all_to_all(
            sent_labels.reshape(groups, cap), "dp", split_axis=0, concat_axis=0, tiled=True
        ),
    )
    got_rows = got_rows.reshape(slots, half)
    got_labels = got_labels.reshape(slots)
    label_hot = got_labels[:, None] == jnp.arange(k2_local)[None, :]
    listed = jnp.any(block_lists[:, :, None] == jnp.arange(BLK_DEV)[None, None, :], axis=1).astype(
        jnp.float32
    )
    allowed = jnp.dot(label_hot.astype(jnp.float32), listed) > 0.5
    mask = jnp.repeat(allowed, BR, axis=1)
    cent_f = level1.astype(jnp.float32)
    norms = jnp.sum(cent_f * cent_f, axis=1)
    partial_value = (
        jnp.dot(got_rows, level1.T, preferred_element_type=jnp.float32) - 0.5 * norms[None, :]
    )
    scores = lax.psum(partial_value, "mp") * scale
    resp = soft_weights(scores, mask)
    num = jnp.dot(resp.T, got_rows, preferred_element_type=jnp.float32)
    weight = jnp.sum(resp.astype(jnp.float32), axis=0)
    new_level1 = ((num + cent_f) / (weight + 1.0)[:, None]).astype(jnp.bfloat16)
    member = label_hot.astype(jnp.bfloat16)
    sums = jnp.dot(member.T, got_rows, preferred_element_type=jnp.float32)
    count = jnp.sum(label_hot.astype(jnp.float32), axis=0)
    new_level2 = ((sums + level2.astype(jnp.float32)) / (count + 1.0)[:, None]).astype(jnp.bfloat16)
    third = level3.astype(jnp.float32)
    norms3 = jnp.sum(third * third, axis=1)
    partial3 = (
        jnp.dot(new_level2, level3.T, preferred_element_type=jnp.float32) - 0.5 * norms3[None, :]
    )
    scores3 = lax.psum(partial3, "mp") * scale
    resp3 = jax.nn.softmax(scores3, axis=1).astype(jnp.bfloat16)
    num3 = jnp.dot(resp3.T, new_level2, preferred_element_type=jnp.float32)
    weight3 = jnp.sum(resp3.astype(jnp.float32), axis=0)
    total3, mass3 = lax.psum((num3, weight3), "dp")
    new_level3 = ((total3 + third) / (mass3 + 1.0)[:, None]).astype(jnp.bfloat16)
    return (new_level1, new_level2, new_level3)


MESH = pl.DeviceIdType.MESH
NT = (((1,), (1,)), ((), ()))


def dot_nt(a, b):
    return lax.dot_general(a, b, NT, preferred_element_type=jnp.float32)


def dot_nn(a, b):
    return jnp.dot(a, b, preferred_element_type=jnp.float32)


def partner_order(groups):
    half = groups // 2
    order = []
    for step in range(half):
        for offset in (half + step, half - step):
            if 0 < offset < groups and offset not in order:
                order.append(offset)
    return [0] + order[::-1]


def step_kernel(
    groups, cap, emb_hbm, lab_ref, lists, l1_hbm, l2_hbm, l3_hbm, o1_hbm, o2_hbm, o3_hbm,
    emb, l1, l2, l3, part3_own, o1, in_sem, out_sem,
    sent, sent_lab, got, got_peer, got_lab, l1_peer, l3_peer, half_norm, half_norm3,
    num, mass, sums, count, listed, n2, n2_peer, part3, w3, got3, got_w3, n3,
    one_send, one_recv, row_send, row_recv, lab_send, lab_recv, fwd_send, fwd_recv,
    sum_send, sum_recv, w_send, w_recv, end_send, end_recv,
):
    me = lax.axis_index("dp")
    other = 1 - lax.axis_index("mp")
    rows = emb.shape[0]
    k2 = l2.shape[0]
    k3 = l3.shape[0]
    k1 = l1.shape[0]
    seg = k3 // groups
    scale = float(E) ** (-0.5)
    order = partner_order(groups)

    def to_owner(offset):
        return lax.rem(me + offset, groups)

    def load(src, dst, index):
        return pltpu.make_async_copy(src, dst, in_sem.at[index])

    emb_load = load(emb_hbm, emb, 0)
    l1_load = load(l1_hbm, l1, 1)
    l2_load = load(l2_hbm, l2, 2)
    l3_load = load(l3_hbm, l3, 3)
    emb_load.start()
    barrier = pltpu.get_barrier_semaphore()
    for offset in range(1, groups):
        pl.semaphore_signal(barrier, inc=1, device_id={"dp": to_owner(offset)}, device_id_type=MESH)
    pl.semaphore_signal(barrier, inc=1, device_id={"mp": other}, device_id_type=MESH)

    l1_load.start()
    l3_load.start()
    l2_load.start()

    label = lab_ref[...].reshape(1, rows)
    at = me + lax.broadcasted_iota(jnp.int32, (groups, rows), 0)
    first = jnp.where(at >= groups, at - groups, at) * k2
    here = (label >= first) & (label < first + k2)
    upper = lax.broadcasted_iota(jnp.int32, (rows, rows), 0) <= lax.broadcasted_iota(
        jnp.int32, (rows, rows), 1
    )
    upper = jnp.where(upper, 1.0, 0.0).astype(jnp.bfloat16)
    cum = dot_nn(jnp.where(here, 1.0, 0.0).astype(jnp.bfloat16), upper).astype(jnp.int32)
    key = jnp.where(here, cum - 1, -1)
    local = jnp.where(here, label - first + 1, 0).astype(jnp.float32)

    def peer_copy(src, dst, index):
        return pltpu.make_async_remote_copy(
            src_ref=src, dst_ref=dst, send_sem=one_send.at[index], recv_sem=one_recv.at[index],
            device_id={"mp": other}, device_id_type=MESH,
        )

    def row_copy(slot, offset):
        return pltpu.make_async_remote_copy(
            src_ref=sent.at[slot], dst_ref=got.at[slot],
            send_sem=row_send.at[slot], recv_sem=row_recv.at[slot],
            device_id={"dp": to_owner(offset)}, device_id_type=MESH,
        )

    def lab_copy(slot, offset):
        return pltpu.make_async_remote_copy(
            src_ref=sent_lab.at[slot], dst_ref=got_lab.at[slot],
            send_sem=lab_send.at[slot], recv_sem=lab_recv.at[slot],
            device_id={"dp": to_owner(offset)}, device_id_type=MESH,
        )

    def forward(slot):
        return pltpu.make_async_remote_copy(
            src_ref=got.at[slot], dst_ref=got_peer.at[slot],
            send_sem=fwd_send.at[slot], recv_sem=fwd_recv.at[slot],
            device_id={"mp": other}, device_id_type=MESH,
        )

    def route(slot):
        offset = order[slot]
        spot = lax.broadcasted_iota(jnp.int32, (128, rows), 0) == key[offset : offset + 1]
        spot = jnp.where(spot, 1.0, 0.0).astype(jnp.bfloat16)
        names = jnp.broadcast_to(local[offset : offset + 1], (8, rows)).astype(jnp.bfloat16)
        return dot_nn(spot[:cap], emb[...]).astype(jnp.bfloat16), dot_nt(names, spot)[0:1]

    emb_load.wait()
    for slot in range(1, groups):
        block, names = route(slot)
        sent[slot] = block
        if slot == 1:
            pl.semaphore_wait(barrier, groups)
        row_copy(slot, order[slot]).start()
        sent_lab[slot] = names
        lab_copy(slot, order[slot]).start()
    l1_copy = peer_copy(l1_hbm, l1_peer, 0)
    l3_copy = peer_copy(l3_hbm, l3_peer, 1)
    block, names = route(0)
    got[0] = block
    got_lab[0] = names
    forward(0).start()
    l1_copy.start()
    l3_copy.start()

    block_of = lax.broadcasted_iota(jnp.int32, (16, k2), 0)
    hit = lists[0:1] == block_of
    for entry in range(1, lists.shape[0]):
        hit = hit | (lists[entry : entry + 1] == block_of)
    listed[...] = jnp.where(hit, 1.0, 0.0).astype(jnp.bfloat16)
    num[...] = jnp.zeros_like(num)
    mass[...] = jnp.zeros_like(mass)
    sums[...] = jnp.zeros_like(sums)
    count[...] = jnp.zeros_like(count)

    def own_norms(x):
        x = x.astype(jnp.float32)
        return 0.5 * jnp.sum(x * x, axis=1, keepdims=True)

    l1_load.wait()
    l3_load.wait()
    l2_load.wait()
    half_norm[...] = own_norms(l1[...])
    norms3 = own_norms(l3[...])
    l1_copy.wait()
    l3_copy.wait()
    half_norm[...] += own_norms(l1_peer[...])
    norms3 = norms3 + own_norms(l3_peer[...])
    half_norm3[...] = jnp.broadcast_to(norms3, (k3, 128)).T

    def hot(slot):
        names = got_lab[slot][0:1, :cap].astype(jnp.int32) - 1
        return lax.broadcasted_iota(jnp.int32, (k2, cap), 0) == names

    def level2_part(slot):
        member = jnp.where(hot(slot), 1.0, 0.0)
        sums[...] += dot_nn(member.astype(jnp.bfloat16), got[slot])
        count[...] += member

    def level1_part(slot):
        own = got[slot]
        peer = got_peer[slot]
        member = jnp.where(hot(slot), 1.0, 0.0).astype(jnp.bfloat16)
        allowed = dot_nn(listed[...], member)
        top = jnp.full((1, cap), -1e30, jnp.float32)
        scores = []
        masks = []
        for b in range(BLK_DEV):
            span = pl.ds(b * BR, BR)
            score = (dot_nt(l1[span], own) + dot_nt(l1_peer[span], peer) - half_norm[span]) * scale
            mask = jnp.broadcast_to(allowed[b : b + 1], (BR, cap)) > 0.5
            top = jnp.maximum(top, jnp.max(jnp.where(mask, score, -1e30), axis=0, keepdims=True))
            scores.append(score)
            masks.append(mask)
        total = jnp.zeros((1, cap), jnp.float32)
        for b in range(BLK_DEV):
            scores[b] = jnp.where(masks[b], jnp.exp(scores[b] - top), 0.0)
            total = total + jnp.sum(scores[b], axis=0, keepdims=True)
        inverse = 1.0 / jnp.where(total > 0, total, 1.0)
        for b in range(BLK_DEV):
            span = pl.ds(b * BR, BR)
            resp = (scores[b] * inverse).astype(jnp.bfloat16)
            num[span] += dot_nn(resp, own)
            mass[span] += resp.astype(jnp.float32)

    level2_part(0)

    def one_slot(slot, carry):
        lab_copy(slot, 0).wait_recv()
        row_copy(slot, 0).wait_recv()
        forward(slot).start()
        level2_part(slot)
        forward(slot - 1).wait_recv()
        level1_part(slot - 1)
        return carry

    lax.fori_loop(1, groups - 1, one_slot, 0)
    last = groups - 1
    lab_copy(last, 0).wait_recv()
    row_copy(last, 0).wait_recv()
    forward(last).start()
    level2_part(last)
    members = jnp.sum(count[...], axis=1, keepdims=True)
    new2 = ((sums[...] + l2[...].astype(jnp.float32)) / (members + 1.0)).astype(jnp.bfloat16)
    n2[...] = new2
    n2_copy = peer_copy(n2, n2_peer, 2)
    n2_copy.start()
    o2_copy = pltpu.make_async_copy(n2, o2_hbm, out_sem.at[BLK_DEV])
    o2_copy.start()
    forward(last - 1).wait_recv()
    level1_part(last - 1)
    n2_copy.wait()

    scores3 = dot_nt(n2[...], l3[...]) + dot_nt(n2_peer[...], l3_peer[...])
    norm_row = half_norm3[...]
    scores3 = (scores3 - norm_row[0:1]) * scale
    top3 = jnp.max(scores3, axis=1, keepdims=True)
    exp3 = jnp.exp(scores3 - top3)
    resp3 = exp3 / jnp.sum(exp3, axis=1, keepdims=True)
    resp3 = resp3.astype(jnp.bfloat16).astype(jnp.float32)
    sum3 = dot_nn(resp3.T.astype(jnp.bfloat16), n2[...])
    part3[...] = sum3.astype(jnp.bfloat16)
    part3_own[...] = sum3
    w3[...] = jnp.sum(resp3, axis=0, keepdims=True)

    def share(owner):
        return pl.ds(pl.multiple_of(owner * seg, seg), seg)

    def sum_copy(slot, offset):
        return pltpu.make_async_remote_copy(
            src_ref=part3.at[share(to_owner(offset))], dst_ref=got3.at[slot],
            send_sem=sum_send.at[slot], recv_sem=sum_recv.at[slot],
            device_id={"dp": to_owner(offset)}, device_id_type=MESH,
        )

    def w_copy(slot, offset):
        return pltpu.make_async_remote_copy(
            src_ref=w3, dst_ref=got_w3.at[slot],
            send_sem=w_send.at[slot], recv_sem=w_recv.at[slot],
            device_id={"dp": to_owner(offset)}, device_id_type=MESH,
        )

    def end_copy(slot, offset):
        return pltpu.make_async_remote_copy(
            src_ref=n3.at[share(me)], dst_ref=n3.at[share(me)],
            send_sem=end_send.at[slot], recv_sem=end_recv.at[slot],
            device_id={"dp": to_owner(offset)}, device_id_type=MESH,
        )

    for slot in range(1, groups):
        w_copy(slot, order[slot]).start()
        sum_copy(slot, order[slot]).start()

    forward(last).wait_recv()
    level1_part(last)
    o1_copies = []
    for b in range(BLK_DEV):
        span = pl.ds(b * BR, BR)
        weight = jnp.sum(mass[span], axis=1, keepdims=True)
        o1[span] = ((num[span] + l1[span].astype(jnp.float32)) / (weight + 1.0)).astype(jnp.bfloat16)
        copy = pltpu.make_async_copy(o1.at[span], o1_hbm.at[span], out_sem.at[b])
        copy.start()
        o1_copies.append(copy)

    total3 = part3_own[share(me)]
    mass3 = w3[...]
    for slot in range(1, groups):
        w_copy(slot, order[slot]).wait_recv()
        sum_copy(slot, order[slot]).wait_recv()
        total3 = total3 + got3[slot].astype(jnp.float32)
        mass3 = mass3 + got_w3[slot]
    mine = lax.broadcasted_iota(jnp.int32, (seg, k3), 1) == me * seg + lax.broadcasted_iota(
        jnp.int32, (seg, k3), 0
    )
    mass_own = jnp.sum(jnp.where(mine, mass3, 0.0), axis=1, keepdims=True)
    new3 = (total3 + l3[share(me)].astype(jnp.float32)) / (mass_own + 1.0)
    n3[share(me)] = new3.astype(jnp.bfloat16)
    for slot in range(1, groups):
        end_copy(slot, order[slot]).start()
    for slot in range(1, groups):
        lab_copy(slot, order[slot]).wait_send()
        row_copy(slot, order[slot]).wait_send()
        w_copy(slot, order[slot]).wait_send()
        sum_copy(slot, order[slot]).wait_send()
    for slot in range(groups):
        forward(slot).wait_send()
    for slot in range(1, groups):
        end_copy(slot, order[slot]).wait_recv()
    o3_copy = pltpu.make_async_copy(n3, o3_hbm, out_sem.at[BLK_DEV + 1])
    o3_copy.start()
    for copy in o1_copies:
        copy.wait()
    o2_copy.wait()
    for slot in range(1, groups):
        end_copy(slot, order[slot]).wait_send()
    o3_copy.wait()


def write_kernel(a, b, c, a_out, b_out, c_out, a_mid, b_mid, c_mid, in_sem, out_sem):
    pieces = []
    for index in range(BLK_DEV):
        span = pl.ds(index * BR, BR)
        pieces.append((a.at[span], a_mid.at[span], a_out.at[span]))
    pieces += [(b, b_mid, b_out), (c, c_mid, c_out)]
    reads, writes = [], []
    for index, (src, mid, dst) in enumerate(pieces):
        reads.append(pltpu.make_async_copy(src, mid, in_sem.at[index]))
        writes.append(pltpu.make_async_copy(mid, dst, out_sem.at[index]))
    for read in reads:
        read.start()
    for read, write in zip(reads, writes):
        read.wait()
        write.start()
    for write in writes:
        write.wait()


def shards(embeddings, labels, block_lists, level1, level2, level3):
    groups = lax.axis_size("dp")
    rows, half = embeddings.shape
    k1, k2, k3 = level1.shape[0], level2.shape[0], level3.shape[0]
    cap = max(2, 2 * rows // groups)
    if cap % 16 or cap > 128 or groups % 8 or k3 % (16 * groups):
        return plain_shards(embeddings, labels, block_lists, level1, level2, level3)
    vmem = pl.BlockSpec(memory_space=pltpu.VMEM)
    hbm = pl.BlockSpec(memory_space=pltpu.HBM)
    bf16, f32 = jnp.bfloat16, jnp.float32
    dma = pltpu.SemaphoreType.DMA
    seg = k3 // groups
    outs = pl.pallas_call(
        functools.partial(step_kernel, groups, cap),
        out_shape=(
            jax.ShapeDtypeStruct((k1, half), bf16),
            jax.ShapeDtypeStruct((k2, half), bf16),
            jax.ShapeDtypeStruct((k3, half), bf16),
        ),
        in_specs=[hbm, vmem, vmem, hbm, hbm, hbm],
        out_specs=(hbm,) * 3,
        scratch_shapes=[
            pltpu.VMEM((rows, half), bf16),
            pltpu.VMEM((k1, half), bf16),
            pltpu.VMEM((k2, half), bf16),
            pltpu.VMEM((k3, half), bf16),
            pltpu.VMEM((k3, half), f32),
            pltpu.VMEM((k1, half), bf16),
            dma((4,)),
            dma((BLK_DEV + 2,)),
            pltpu.VMEM((groups, cap, half), bf16),
            pltpu.VMEM((groups, 1, 128), f32),
            pltpu.VMEM((groups, cap, half), bf16),
            pltpu.VMEM((groups, cap, half), bf16),
            pltpu.VMEM((groups, 1, 128), f32),
            pltpu.VMEM((k1, half), bf16),
            pltpu.VMEM((k3, half), bf16),
            pltpu.VMEM((k1, 1), f32),
            pltpu.VMEM((128, k3), f32),
            pltpu.VMEM((k1, half), f32),
            pltpu.VMEM((k1, cap), f32),
            pltpu.VMEM((k2, half), f32),
            pltpu.VMEM((k2, cap), f32),
            pltpu.VMEM((16, k2), bf16),
            pltpu.VMEM((k2, half), bf16),
            pltpu.VMEM((k2, half), bf16),
            pltpu.VMEM((k3, half), bf16),
            pltpu.VMEM((1, k3), f32),
            pltpu.VMEM((groups, seg, half), bf16),
            pltpu.VMEM((groups, 1, k3), f32),
            pltpu.VMEM((k3, half), bf16),
            dma((3,)),
            dma((3,)),
        ]
        + [dma((groups,))] * 12,
        compiler_params=pltpu.CompilerParams(
            collective_id=0, has_side_effects=True, vmem_limit_bytes=60 * 1024 * 1024
        ),
    )(embeddings, labels, block_lists.T, level1, level2, level3)
    return pl.pallas_call(
        write_kernel,
        out_shape=tuple(jax.ShapeDtypeStruct(out.shape, out.dtype) for out in outs),
        in_specs=[hbm] * 3,
        out_specs=(hbm,) * 3,
        scratch_shapes=[pltpu.VMEM(out.shape, out.dtype) for out in outs]
        + [dma((BLK_DEV + 2,))] * 2,
        compiler_params=pltpu.CompilerParams(vmem_limit_bytes=60 * 1024 * 1024),
    )(*outs)


def solution(mesh):
    return jax.shard_map(
        shards,
        mesh=mesh,
        in_specs=(
            P(("parts", "dp"), "mp"),
            P(("parts", "dp")),
            P(("parts", "dp"), None),
            P(("parts", "dp"), "mp"),
            P(("parts", "dp"), "mp"),
            P("parts", "mp"),
        ),
        out_specs=(P(("parts", "dp"), "mp"), P(("parts", "dp"), "mp"), P("parts", "mp")),
        check_vma=False,
    )
```
